128 devices in a mesh: tok: 32 (over y, x, core), head: 4 (over z).
Axes of the slice: x: 4, y: 4, z: 4, core: 2. Of those that a mesh axis runs over, the one named last changes fastest.
Arguments:
- queries: bfloat16 [49152, 1536], P('tok', 'head'), may hold values from -6 to 6
- keys: bfloat16 [49152, 1536], P('tok', 'head'), may hold values from -6 to 6
- values: bfloat16 [49152, 1536], P('tok', 'head'), may hold values from -6 to 6
- clusters: int32 [12, 49152], P('head', 'tok'), may hold values from 0 to 127, as said below
- cluster_slot: int32 [12, 128], P('head'), may hold values from 0 to 127, as said below
- pair_shift: int32 [12, 128], P('head'), may hold values from 1 to 3
- w_out: bfloat16 [1536, 3072], P('head'), may hold values from -1.8359375 to 1.8359375
Outputs:
- mixed: bfloat16 [49152, 3072], P('tok', 'head')
The draws below stay inside these ranges and needn't reach their ends.
Inputs may be any that keep to these rules, and one draw needn't show every extreme that they name: For each head, each device's block of 1536 tokens holds at most 36 tokens of one cluster and at most 96 tokens of the clusters held by one device. In every head one cluster has exactly 36 tokens in every block, so 1152 in all, and in every block some holding device gets exactly 96. In a block, a cluster's count is a positive multiple of 6, and the holding devices get 96 tokens for a quarter of them, 48 for another quarter and 24 for the rest. In each head cluster_slot is a permutation of the clusters, and the group of cluster c (cluster_slot[h, c] // 4) is held by the device of tok with that index.
All inputs are finite; a program needn't handle non-finite values.
Results may differ from the reference program's by a relative error of at most 0.013.
Values may be sent and summed in bfloat16 or wider, within the bound.
A program may use at most 128 MiB of HBM per device.

```python
import math
import jax
import jax.numpy as jnp
import numpy as np
from jax import lax

D = 3072
HD = 128
HEADS = 12
CL_DEV = 4
TOK_DEV = 1536
TOKENS = 49152
HEAD_DEV = 3
CLUSTERS = 128
CAPC = 1152
N_HEAD = 4


def block_pattern(peer_count):
    unit_rows = TOK_DEV // peer_count // 8
    shares = np.array([[6, 6, 2, 2], [4, 2, 1, 1], [1, 1, 1, 1], [1, 1, 1, 1]])
    levels = np.arange(peer_count) // (peer_count // 4)
    counts = (shares[levels] * unit_rows).reshape(-1)
    rank_list = np.repeat(np.repeat(np.arange(peer_count), 4), counts)
    local_list = np.repeat(np.tile(np.arange(4), peer_count), counts)
    return (rank_list, local_list)


def put_first(order, wanted):
    where_now = jnp.argmax(order == wanted)
    return order.at[where_now].set(order[0]).at[0].set(wanted)


def layout(key):
    peer_count = TOKENS // TOK_DEV
    rank_list, local_list = block_pattern(peer_count)

    def per_head(head_key):
        table_key, star_key, local_key, blocks_key = jax.random.split(head_key, 4)
        cluster_at = jax.random.permutation(table_key, CLUSTERS)
        star_owner = jax.random.randint(star_key, (), 0, peer_count)
        star_local = jax.random.randint(local_key, (), 0, CL_DEV)

        def per_block(block_key):
            owner_key, locals_key, shuffle_key = jax.random.split(block_key, 3)
            owners = put_first(jax.random.permutation(owner_key, peer_count), star_owner)
            local_orders = jax.vmap(lambda each_key: jax.random.permutation(each_key, CL_DEV))(jax.random.split(locals_key, peer_count))
            starred = jax.vmap(lambda each_row: put_first(each_row, star_local))(local_orders)
            local_orders = jnp.where((owners == star_owner)[:, None], starred, local_orders)
            slots = owners[rank_list] * CL_DEV + local_orders[rank_list, local_list]
            shuffle = jax.random.permutation(shuffle_key, TOK_DEV)
            inverse = jnp.argsort(shuffle)
            return (cluster_at[slots][shuffle], inverse[:2])
        labels, chosen = jax.vmap(per_block)(jax.random.split(blocks_key, peer_count))
        return (labels.reshape(-1), jnp.argsort(cluster_at), chosen)
    return jax.vmap(per_head)(jax.random.split(key, HEADS))


def draw_clusters(key, part):
    labels, slot_of, chosen = layout(key)
    return labels.astype(jnp.int32)


def draw_cluster_slot(key, part):
    labels, slot_of, chosen = layout(key)
    return slot_of.astype(jnp.int32)


def draw_queries(key, part):
    key = jax.random.fold_in(key, 11)
    drawn = jnp.clip(jax.random.normal(key, (TOKENS, HEADS * HD), jnp.float32), -6.0, 6.0)
    return drawn.astype(jnp.bfloat16)


def draw_keys(key, part):
    key = jax.random.fold_in(key, 23)
    drawn = jnp.clip(jax.random.normal(key, (TOKENS, HEADS * HD), jnp.float32), -6.0, 6.0)
    return drawn.astype(jnp.bfloat16)


def set_ends(values, stream_key, low, largest):
    spot = [jax.random.randint(jax.random.fold_in(stream_key, axis), (), 0, length) for axis, length in enumerate(values.shape)]
    widest = values.shape.index(max(values.shape))
    beside = spot[:widest] + [(spot[widest] + 1) % values.shape[widest]] + spot[widest + 1:]
    return values.at[tuple(spot)].set(low).at[tuple(beside)].set(largest)


def block_levels(key, shape, cuts, low, high):
    def one(axis_at, blocks):
        heights = jax.random.uniform(jax.random.fold_in(jax.random.fold_in(key, 6), axis_at), (blocks,), jnp.float32, low / len(cuts), high / len(cuts))
        return jnp.repeat(jnp.exp(heights), shape[axis_at] // blocks).reshape((-1,) + (1,) * (len(shape) - axis_at - 1))

    gain = one(*cuts[0])
    for cut in cuts[1:]:
        gain = gain * one(*cut)
    return gain


def centred(rng, dims, deviation, bound, cuts=(), held_as=jnp.bfloat16):
    gain = block_levels(rng, dims, cuts, -0.22, 0.18) if cuts else 1.0
    values = jax.random.normal(rng, dims, jnp.float32) * deviation * gain
    return jnp.minimum(jnp.maximum(values, -bound), bound).astype(held_as)


def setup_inputs(seed: int = 0) -> dict:
    seeds = jax.random.split(jax.random.key(seed), 8)
    queries = draw_queries(jax.random.fold_in(seeds[7], 71), 0)
    keys = draw_keys(jax.random.fold_in(seeds[7], 71), 0)
    values = centred(seeds[2], (TOKENS, HEADS * HD), 1.0, 6.0, ((0, 32), (1, 4)))
    clusters = draw_clusters(jax.random.fold_in(seeds[7], 71), 0)
    cluster_slot = draw_cluster_slot(jax.random.fold_in(seeds[7], 71), 0)
    pair_shift = set_ends(jax.random.randint(seeds[5], (HEADS, CLUSTERS), 1, CL_DEV), jax.random.fold_in(seeds[5], 1), 1, CL_DEV - 1).astype(jnp.int32)
    w_out = centred(seeds[6], (HEADS * HD, D), (12.0 / (HEADS * HD) ** 0.5), 1.8359375, ((0, 4),))
    return {"queries": queries, "keys": keys, "values": values, "clusters": clusters, "cluster_slot": cluster_slot, "pair_shift": pair_shift, "w_out": w_out}


def normalized(query_rows, key_rows, value_rows, usable):
    scores = jnp.dot(query_rows, key_rows.T, preferred_element_type=jnp.float32) / math.sqrt(HD)
    scores = jnp.where(usable, scores, -jnp.inf)
    row_max = lax.optimization_barrier(jnp.max(scores, axis=1, keepdims=True))
    expd_values = jnp.exp(scores - row_max)
    row_total = lax.optimization_barrier(jnp.sum(expd_values, axis=1, keepdims=True))
    weights = expd_values.astype(jnp.bfloat16)
    summed = jnp.dot(weights, value_rows, preferred_element_type=jnp.float32)
    return (summed / row_total).astype(jnp.bfloat16)

def one_head(query_head, key_head, value_head, labels, slot_row, shift_row):
    token_count = query_head.shape[0]
    slot_mate = slot_row // CL_DEV * CL_DEV + (slot_row % CL_DEV + shift_row) % CL_DEV
    cluster_at = jnp.zeros((CLUSTERS,), jnp.int32).at[slot_row].set(jnp.arange(CLUSTERS, dtype=jnp.int32))
    partner = cluster_at[slot_mate].astype(jnp.int32)
    sorted_idx = jnp.argsort(labels, stable=True).astype(jnp.int32)
    counts = jnp.zeros((CLUSTERS,), jnp.int32).at[labels].add(1)
    starts = (jnp.cumsum(counts) - counts).astype(jnp.int32)
    padded_idx = jnp.concatenate([sorted_idx, jnp.zeros((CAPC,), jnp.int32)])
    capacity_rows = jnp.arange(CAPC, dtype=jnp.int32)

    def per_cluster(cluster_index):
        own_rows = lax.dynamic_slice(padded_idx, (starts[cluster_index],), (CAPC,))
        mate_cluster = partner[cluster_index]
        mate_rows = lax.dynamic_slice(padded_idx, (starts[mate_cluster],), (CAPC,))
        usable = jnp.concatenate([capacity_rows < counts[cluster_index], capacity_rows < counts[mate_cluster]])
        key_index = jnp.concatenate([own_rows, mate_rows])
        return normalized(query_head[own_rows], key_head[key_index], value_head[key_index], usable[None, :])
    results = lax.map(per_cluster, jnp.arange(CLUSTERS, dtype=jnp.int32))
    filled = capacity_rows[None, :] < counts[:, None]
    targets = jnp.where(filled, starts[:, None] + capacity_rows[None, :], token_count).astype(jnp.int32)
    sorted_out = jnp.zeros((token_count + 1, HD), results.dtype).at[targets.reshape(-1)].set(results.reshape(-1, HD))
    return jnp.zeros((token_count, HD), results.dtype).at[sorted_idx].set(sorted_out[:token_count])

def reference(queries, keys, values, clusters, cluster_slot, pair_shift, w_out):
    token_count = queries.shape[0]
    head_outputs = []
    for head_index in range(HEADS):
        start_col = head_index * HD
        head_outputs.append(one_head(queries[:, start_col:start_col + HD], keys[:, start_col:start_col + HD], values[:, start_col:start_col + HD], clusters[head_index], cluster_slot[head_index], pair_shift[head_index]))
    attention = jnp.concatenate(head_outputs, axis=1)
    group_cols = HEAD_DEV * HD
    mixed = jnp.zeros((token_count, D), jnp.float32)
    for group_index in range(N_HEAD):
        lower = group_index * group_cols
        piece_term = jnp.dot(attention[:, lower:lower + group_cols], w_out[lower:lower + group_cols], preferred_element_type=jnp.float32)
        piece_term = lax.optimization_barrier(piece_term.astype(jnp.bfloat16))
        mixed = mixed + piece_term.astype(jnp.float32)
    return mixed.astype(jnp.bfloat16)
```

```python
import math

import jax
import jax.numpy as jnp
from jax import lax
from jax.experimental import pallas as pl
from jax.experimental.pallas import tpu as pltpu
from jax.sharding import PartitionSpec as P

HD = 128
CL_DEV = 4
SLOTS = 128
HEADS = 3
PEERS = 32
PLANES = 4
TOK = 1536
BOX = 96
ROWS = PEERS * BOX
OUT = 768
QUAD = 4 * BOX
BIG = 1e30
SCALE = math.log2(math.e) / math.sqrt(HD)
MESH = pl.DeviceIdType.MESH
F32 = jnp.float32
BF16 = jnp.bfloat16


def iota(shape, dim):
    return lax.broadcasted_iota(jnp.int32, shape, dim)


def dot(left, right):
    return jnp.dot(left, right, preferred_element_type=F32)


def dot_t(left, right):
    return lax.dot_general(
        left, right, (((1,), (1,)), ((), ())), preferred_element_type=F32
    )


def kernel(
    q_ref, k_ref, v_ref, cl_ref, slot_ref, shift_ref, w_ref, out_ref,
    outbox, inbox, msg_out, msg_in, ret_out, ret_in, att, wcol, acc,
    pos_row, pos_all, qa, ka, va, allow,
    box_send, box_recv, msg_send, msg_recv, ret_send, ret_recv,
    att_send, att_recv, w_send, w_recv, w_own,
):
    me = lax.axis_index("tok")
    plane = lax.axis_index("head")
    core, chip = me % 2, me // 2
    x, y = chip % 4, chip // 4

    def device(there_y, there_x, there_core):
        return (there_y * 4 + there_x) * 2 + there_core

    def seat(there_y, there_x, there_core):
        return there_core * 16 + there_y * 4 + there_x

    my_seat = seat(y, x, core)

    barrier = pltpu.get_barrier_semaphore()
    for step in range(1, PEERS):
        pl.semaphore_signal(
            barrier, inc=1, device_id=((me + step) % PEERS, plane), device_id_type=MESH
        )
    for step in range(1, PLANES):
        pl.semaphore_signal(
            barrier, inc=1, device_id=(me, (plane + step) % PLANES), device_id_type=MESH
        )

    below = (iota((128, 128), 0) <= iota((128, 128), 1)).astype(BF16)
    ones = jnp.ones((128, 128), BF16)
    row_id, col_id = iota((128, 128), 0), iota((128, 128), 1)
    same = row_id // CL_DEV == col_id // CL_DEV
    before = (same & (col_id < row_id)).astype(BF16)
    after = (same & (row_id < col_id)).astype(BF16)
    box_base = (row_id // CL_DEV * BOX - 1).astype(F32)
    for h in range(HEADS):
        slot_line = slot_ref[h : h + 1, :]
        of_cluster = (iota((SLOTS, TOK), 0) == cl_ref[h : h + 1, :]).astype(BF16)
        slot_rows = jnp.broadcast_to(slot_line.astype(F32), (8, SLOTS)).astype(BF16)
        token_slot = dot(slot_rows, of_cluster)[0:1].astype(jnp.int32)
        hot = iota((SLOTS, TOK), 0) == token_slot
        hot_f, hot_b = hot.astype(F32), hot.astype(BF16)
        counted = jnp.zeros((128, 128), F32)
        within = []
        for b in range(TOK // 128):
            block = hot_b[:, b * 128 : (b + 1) * 128]
            within.append(dot(block, below) + counted)
            counted = counted + dot(block, ones)
        start = dot(before, counted.astype(BF16)) + box_base
        for b in range(TOK // 128):
            lanes = slice(b * 128, (b + 1) * 128)
            line = jnp.sum(hot_f[:, lanes] * (within[b] + start), axis=0, keepdims=True)
            pos_row[h : h + 1, lanes] = line
            pos_all[h, lanes, :] = jnp.broadcast_to(line, (128, 128)).T
        count_line = dot_t(jnp.ones((8, TOK), BF16), hot_b)
        low = dot(count_line.astype(BF16), after)
        msg_out[2 * h : 2 * h + 1, :] = low[0:1]
        msg_out[2 * h + 1 : 2 * h + 2, :] = (low + count_line)[0:1]
        placed = (row_id == slot_line).astype(BF16)
        shift_rows = jnp.broadcast_to(shift_ref[h : h + 1, :].astype(F32), (8, SLOTS))
        shift = dot_t(shift_rows.astype(BF16), placed)[0:1].astype(jnp.int32)
        mate = col_id // CL_DEV * CL_DEV + (col_id % CL_DEV + shift) % CL_DEV
        allow[h] = ((row_id == col_id) | (row_id == mate)).astype(BF16)
    msg_out[6:8, :] = jnp.zeros((2, 128), F32)
    msg_in[my_seat] = msg_out[...]

    pl.semaphore_wait(barrier, PEERS - 1 + PLANES - 1)

    own_w = pltpu.make_async_copy(
        w_ref.at[:, pl.ds(pl.multiple_of(plane * OUT, 128), OUT)], wcol.at[plane], w_own
    )
    own_w.start()
    w_copies = []
    for step in range(1, PLANES):
        there = (plane + step) % PLANES
        copy = pltpu.make_async_remote_copy(
            src_ref=w_ref.at[:, pl.ds(pl.multiple_of(there * OUT, 128), OUT)],
            dst_ref=wcol.at[plane],
            send_sem=w_send.at[step - 1],
            recv_sem=w_recv.at[step - 1],
            device_id=(me, there),
            device_id_type=MESH,
        )
        copy.start()
        w_copies.append(copy)

    def peer_of(g, j):
        return device((y + 2 * g + j // 4 + j) % 4, (x + j) % 4, (core + g // 2) % 2)

    for h in range(HEADS):
        cols = slice(h * HD, (h + 1) * HD)

        def pack(g, _, h=h, cols=cols):
            pos = pos_row[h : h + 1, :].astype(jnp.int32)
            picks = []
            for j in range(8):
                picks.append((iota((BOX, TOK), 0) + peer_of(g, j) * BOX == pos).astype(BF16))
            pick = jnp.concatenate(picks, axis=0)
            rows = jnp.concatenate([q_ref[:, cols], k_ref[:, cols], v_ref[:, cols]], axis=1)
            base = pl.multiple_of(g * 8 * BOX, 8 * BOX)
            outbox[h, pl.ds(base, 8 * BOX), :] = dot(pick, rows).astype(BF16)
            for j in range(8):
                def send(g=g, j=j):
                    peer = (peer_of(g, j), plane)
                    k = g * 8 + j
                    pltpu.make_async_remote_copy(
                        src_ref=outbox.at[h, pl.ds(pl.multiple_of(k * BOX, BOX), BOX)],
                        dst_ref=inbox.at[h, pl.ds(pl.multiple_of(my_seat * BOX, BOX), BOX)],
                        send_sem=box_send.at[h],
                        recv_sem=box_recv.at[h],
                        device_id=peer,
                        device_id_type=MESH,
                    ).start()
                    if h == 0:
                        pltpu.make_async_remote_copy(
                            src_ref=msg_out,
                            dst_ref=msg_in.at[my_seat],
                            send_sem=msg_send,
                            recv_sem=msg_recv,
                            device_id=peer,
                            device_id_type=MESH,
                        ).start()
                if j == 0:
                    pl.when(g != 0)(send)
                else:
                    send()
            return 0

        lax.fori_loop(0, 4, pack, 0)
        inbox[h, pl.ds(pl.multiple_of(my_seat * BOX, BOX), BOX), :] = outbox[h, 0:BOX, :]

    va[:, HD:] = jnp.ones((ROWS, HD), BF16)

    def wait_bytes(ref, semaphore):
        pltpu.make_async_copy(ref, ref, semaphore).wait()

    others = (PEERS - 1) * BOX

    def attend(h):
        wait_bytes(inbox.at[h, pl.ds(0, others)], box_recv.at[h])
        if h == 0:
            wait_bytes(msg_in.at[pl.ds(0, PEERS - 1)], msg_recv)

        def prepare(s, _):
            base = pl.multiple_of(s * QUAD, QUAD)
            at = iota((BOX, SLOTS), 0).astype(F32)
            mine = iota((BOX, SLOTS), 1) // CL_DEV == me
            tags = []
            for j in range(4):
                low = msg_in[s * 4 + j, 2 * h : 2 * h + 1, :]
                high = msg_in[s * 4 + j, 2 * h + 1 : 2 * h + 2, :]
                tags.append(((at >= low) & (at < high) & mine).astype(BF16))
            tag = jnp.concatenate(tags, axis=0)
            box = inbox[h, pl.ds(base, QUAD), :]
            qa[pl.ds(base, QUAD), 0:HD] = box[:, 0:HD]
            qa[pl.ds(base, QUAD), HD:] = tag
            ka[pl.ds(base, QUAD), 0:HD] = box[:, HD : 2 * HD]
            ka[pl.ds(base, QUAD), HD:] = ((dot(tag, allow[h]) - 1.0) * BIG).astype(BF16)
            va[pl.ds(base, QUAD), 0:HD] = box[:, 2 * HD :]
            return 0

        lax.fori_loop(0, PEERS // 4, prepare, 0)

        def chunk(c, _):
            there_core, there_y = c // 4, (y + c % 4) % 4
            base = pl.multiple_of(seat(there_y, 0, there_core) * BOX, QUAD)
            scores = dot_t(qa[pl.ds(base, QUAD), :], ka[...])
            top = jnp.max(scores, axis=1, keepdims=True)
            weights = jnp.exp2((scores - top) * SCALE).astype(BF16)
            summed = dot(weights, va[...])
            ret_out[h, pl.ds(base, QUAD), :] = (summed[:, :HD] / summed[:, HD:]).astype(BF16)
            mine = pl.ds(pl.multiple_of(me * BOX, BOX), BOX)
            for j in range(4):
                there_x = (x + j) % 4
                rows = pl.ds(pl.multiple_of(base + there_x * BOX, BOX), BOX)

                def send(rows=rows, there_x=there_x):
                    pltpu.make_async_remote_copy(
                        src_ref=ret_out.at[h, rows],
                        dst_ref=ret_in.at[h, mine],
                        send_sem=ret_send.at[h],
                        recv_sem=ret_recv.at[h],
                        device_id=(device(there_y, there_x, there_core), plane),
                        device_id_type=MESH,
                    ).start()

                if j == 0:
                    self_here = (c % 4 == 0) & (there_core == core)
                    pl.when(jnp.logical_not(self_here))(send)

                    def keep(rows=rows):
                        ret_in[h, mine, :] = ret_out[h, rows, :]

                    pl.when(self_here)(keep)
                else:
                    send()
            return 0

        lax.fori_loop(0, 8, chunk, 0)

    att_copies = {}

    def restore(h):
        wait_bytes(ret_in.at[h, pl.ds(0, others)], ret_recv.at[h])

        def tokens(c, _):
            base = pl.multiple_of(c * QUAD, QUAD)
            pos = pos_all[h, pl.ds(base, QUAD), :].astype(jnp.int32)
            lane = iota((QUAD, 128), 1)
            pick = jnp.concatenate(
                [(pos == lane + b * 128).astype(BF16) for b in range(ROWS // 128)], axis=1
            )
            att[h, plane, pl.ds(base, QUAD), :] = dot(pick, ret_in[h]).astype(BF16)
            return 0

        lax.fori_loop(0, TOK // QUAD, tokens, 0)
        for step in range(1, PLANES):
            copy = pltpu.make_async_remote_copy(
                src_ref=att.at[h, plane],
                dst_ref=att.at[h, plane],
                send_sem=att_send.at[h, step - 1],
                recv_sem=att_recv.at[h, step - 1],
                device_id=(me, (plane + step) % PLANES),
                device_id_type=MESH,
            )
            copy.start()
            att_copies[h, step] = copy

    attend(0)
    attend(1)
    restore(0)
    attend(2)
    restore(1)
    own_w.wait()
    for copy in w_copies:
        copy.wait()
    for h in range(2):
        for step in range(1, PLANES):
            att_copies[h, step].wait_recv()

    def project_two(c, _):
        rows = pl.ds(pl.multiple_of(c * QUAD, QUAD), QUAD)
        total = jnp.zeros((QUAD, OUT), F32)
        for p in range(PLANES):
            pair = jnp.concatenate([att[0, p, rows, :], att[1, p, rows, :]], axis=1)
            total = total + dot(pair, wcol[p, 0 : 2 * HD, :])
        acc[rows, :] = total
        return 0

    lax.fori_loop(0, TOK // QUAD, project_two, 0)
    restore(2)
    for step in range(1, PLANES):
        att_copies[2, step].wait_recv()

    def project_last(c, _):
        rows = pl.ds(pl.multiple_of(c * QUAD, QUAD), QUAD)
        total = acc[rows, :]
        for p in range(0, PLANES, 2):
            pair = jnp.concatenate([att[2, p, rows, :], att[2, p + 1, rows, :]], axis=1)
            both = jnp.concatenate([wcol[p, 2 * HD :, :], wcol[p + 1, 2 * HD :, :]], axis=0)
            total = total + dot(pair, both)
        out_ref[rows, :] = total.astype(BF16)
        return 0

    lax.fori_loop(0, TOK // QUAD, project_last, 0)

    for h in range(HEADS):
        wait_bytes(outbox.at[h, pl.ds(0, others)], box_send.at[h])
        wait_bytes(ret_out.at[h, pl.ds(0, others)], ret_send.at[h])
        for step in range(1, PLANES):
            att_copies[h, step].wait_send()
    wait_bytes(msg_in.at[pl.ds(0, PEERS - 1)], msg_send)


def shards(queries, keys, values, clusters, cluster_slot, pair_shift, w_out):
    vmem = pl.BlockSpec(memory_space=pltpu.VMEM)
    dma = pltpu.SemaphoreType.DMA
    return pl.pallas_call(
        kernel,
        out_shape=jax.ShapeDtypeStruct((TOK, OUT), BF16),
        in_specs=[vmem] * 6 + [pl.BlockSpec(memory_space=pl.ANY)],
        out_specs=vmem,
        scratch_shapes=[
            pltpu.VMEM((HEADS, ROWS, 3 * HD), BF16),
            pltpu.VMEM((HEADS, ROWS, 3 * HD), BF16),
            pltpu.VMEM((8, SLOTS), F32),
            pltpu.VMEM((PEERS, 8, SLOTS), F32),
            pltpu.VMEM((HEADS, ROWS, HD), BF16),
            pltpu.VMEM((HEADS, ROWS, HD), BF16),
            pltpu.VMEM((HEADS, PLANES, TOK, HD), BF16),
            pltpu.VMEM((PLANES, HEADS * HD, OUT), BF16),
            pltpu.VMEM((TOK, OUT), F32),
            pltpu.VMEM((8, TOK), F32),
            pltpu.VMEM((HEADS, TOK, 128), F32),
            pltpu.VMEM((ROWS, 2 * HD), BF16),
            pltpu.VMEM((ROWS, 2 * HD), BF16),
            pltpu.VMEM((ROWS, 2 * HD), BF16),
            pltpu.VMEM((HEADS, SLOTS, SLOTS), BF16),
            dma((HEADS,)),
            dma((HEADS,)),
            dma,
            dma,
            dma((HEADS,)),
            dma((HEADS,)),
            dma((HEADS, PLANES - 1)),
            dma((HEADS, PLANES - 1)),
            dma((PLANES - 1,)),
            dma((PLANES - 1,)),
            dma,
        ],
        compiler_params=pltpu.CompilerParams(
            collective_id=0, has_side_effects=True, vmem_limit_bytes=62 * 2**20
        ),
        cost_estimate=pl.CostEstimate(
            flops=40 * 10**9, bytes_accessed=10 * 10**6, transcendentals=28 * 10**6
        ),
    )(queries, keys, values, clusters, cluster_slot, pair_shift, w_out)


def solution(mesh):
    in_specs = (
        P("tok", "head"),
        P("tok", "head"),
        P("tok", "head"),
        P("head", "tok"),
        P("head", None),
        P("head", None),
        P("head", None),
    )
    return jax.shard_map(
        shards, mesh=mesh, in_specs=in_specs, out_specs=P("tok", "head"), check_vma=False
    )
```

```python
import math

import jax
import jax.numpy as jnp
from jax import lax
from jax.experimental import pallas as pl
from jax.experimental.pallas import tpu as pltpu
from jax.sharding import PartitionSpec as P

HD = 128
CL_DEV = 4
SLOTS = 128
HEADS = 3
PEERS = 32
PLANES = 4
TOK = 1536
BOX = 96
ROWS = PEERS * BOX
OUT = 768
QUAD = 4 * BOX
BIG = 1e30
SCALE = math.log2(math.e) / math.sqrt(HD)
MESH = pl.DeviceIdType.MESH
F32 = jnp.float32
BF16 = jnp.bfloat16


def iota(shape, dim):
    return lax.broadcasted_iota(jnp.int32, shape, dim)


def dot(left, right):
    return jnp.dot(left, right, preferred_element_type=F32)


def dot_t(left, right):
    return lax.dot_general(
        left, right, (((1,), (1,)), ((), ())), preferred_element_type=F32
    )


def kernel(
    q_ref, k_ref, v_ref, cl_ref, slot_ref, shift_ref, w_ref, out_ref,
    outbox, inbox, msg_out, msg_in, ret_out, ret_in, att, wcol, acc,
    pos_row, pos_all, qa, ka, va, allow,
    box_send, box_recv, msg_send, msg_recv, ret_send, ret_recv,
    att_send, att_recv, w_send, w_recv, w_own,
):
    me = lax.axis_index("tok")
    plane = lax.axis_index("head")
    core, chip = me % 2, me // 2
    x, y = chip % 4, chip // 4

    def device(there_y, there_x, there_core):
        return (there_y * 4 + there_x) * 2 + there_core

    def seat(there_y, there_x, there_core):
        return there_core * 16 + there_y * 4 + there_x

    my_seat = seat(y, x, core)

    barrier = pltpu.get_barrier_semaphore()
    for step in range(1, PEERS):
        pl.semaphore_signal(
            barrier, inc=1, device_id=((me + step) % PEERS, plane), device_id_type=MESH
        )
    for step in range(1, PLANES):
        pl.semaphore_signal(
            barrier, inc=1, device_id=(me, (plane + step) % PLANES), device_id_type=MESH
        )

    below = (iota((128, 128), 0) <= iota((128, 128), 1)).astype(BF16)
    ones = jnp.ones((128, 128), BF16)
    row_id, col_id = iota((128, 128), 0), iota((128, 128), 1)
    same = row_id // CL_DEV == col_id // CL_DEV
    before = (same & (col_id < row_id)).astype(BF16)
    after = (same & (row_id < col_id)).astype(BF16)
    box_base = (row_id // CL_DEV * BOX - 1).astype(F32)
    for h in range(HEADS):
        slot_line = slot_ref[h : h + 1, :]
        of_cluster = (iota((SLOTS, TOK), 0) == cl_ref[h : h + 1, :]).astype(BF16)
        slot_rows = jnp.broadcast_to(slot_line.astype(F32), (8, SLOTS)).astype(BF16)
        token_slot = dot(slot_rows, of_cluster)[0:1].astype(jnp.int32)
        hot = iota((SLOTS, TOK), 0) == token_slot
        hot_f, hot_b = hot.astype(F32), hot.astype(BF16)
        counted = jnp.zeros((128, 128), F32)
        within = []
        for b in range(TOK // 128):
            block = hot_b[:, b * 128 : (b + 1) * 128]
            within.append(dot(block, below) + counted)
            counted = counted + dot(block, ones)
        start = dot(before, counted.astype(BF16)) + box_base
        for b in range(TOK // 128):
            lanes = slice(b * 128, (b + 1) * 128)
            line = jnp.sum(hot_f[:, lanes] * (within[b] + start), axis=0, keepdims=True)
            pos_row[h : h + 1, lanes] = line
            pos_all[h, lanes, :] = jnp.broadcast_to(line, (128, 128)).T
        count_line = dot_t(jnp.ones((8, TOK), BF16), hot_b)
        low = dot(count_line.astype(BF16), after)
        msg_out[2 * h : 2 * h + 1, :] = low[0:1]
        msg_out[2 * h + 1 : 2 * h + 2, :] = (low + count_line)[0:1]
        placed = (row_id == slot_line).astype(BF16)
        shift_rows = jnp.broadcast_to(shift_ref[h : h + 1, :].astype(F32), (8, SLOTS))
        shift = dot_t(shift_rows.astype(BF16), placed)[0:1].astype(jnp.int32)
        mate = col_id // CL_DEV * CL_DEV + (col_id % CL_DEV + shift) % CL_DEV
        allow[h] = ((row_id == col_id) | (row_id == mate)).astype(BF16)
    msg_out[6:8, :] = jnp.zeros((2, 128), F32)
    msg_in[my_seat] = msg_out[...]

    pl.semaphore_wait(barrier, PEERS - 1 + PLANES - 1)

    own_w = pltpu.make_async_copy(
        w_ref.at[:, pl.ds(pl.multiple_of(plane * OUT, 128), OUT)], wcol.at[plane], w_own
    )
    own_w.start()
    w_copies = []
    for step in range(1, PLANES):
        there = (plane + step) % PLANES
        copy = pltpu.make_async_remote_copy(
            src_ref=w_ref.at[:, pl.ds(pl.multiple_of(there * OUT, 128), OUT)],
            dst_ref=wcol.at[plane],
            send_sem=w_send.at[step - 1],
            recv_sem=w_recv.at[step - 1],
            device_id=(me, there),
            device_id_type=MESH,
        )
        copy.start()
        w_copies.append(copy)

    def peer_of(g, j):
        return device((y + 2 * g + j // 4 + j) % 4, (x + j) % 4, (core + g // 2) % 2)

    def send_boxes(h, g):
        for j in range(8):
            def send(j=j):
                peer = (peer_of(g, j), plane)
                k = g * 8 + j
                pltpu.make_async_remote_copy(
                    src_ref=outbox.at[h, pl.ds(pl.multiple_of(k * BOX, BOX), BOX)],
                    dst_ref=inbox.at[h, pl.ds(pl.multiple_of(my_seat * BOX, BOX), BOX)],
                    send_sem=box_send.at[h],
                    recv_sem=box_recv.at[h],
                    device_id=peer,
                    device_id_type=MESH,
                ).start()
                if h == 0:
                    pltpu.make_async_remote_copy(
                        src_ref=msg_out,
                        dst_ref=msg_in.at[my_seat],
                        send_sem=msg_send,
                        recv_sem=msg_recv,
                        device_id=peer,
                        device_id_type=MESH,
                    ).start()

            if j == 0:
                pl.when(g != 0)(send)
            else:
                send()

    def send_late(low, high):
        def group(g, _):
            send_boxes(HEADS - 1, g)
            return 0

        lax.fori_loop(low, high, group, 0)

    for h in range(HEADS):
        cols = slice(h * HD, (h + 1) * HD)

        def pack(g, _, h=h, cols=cols):
            pos = pos_row[h : h + 1, :].astype(jnp.int32)
            picks = []
            for j in range(8):
                picks.append((iota((BOX, TOK), 0) + peer_of(g, j) * BOX == pos).astype(BF16))
            pick = jnp.concatenate(picks, axis=0)
            rows = jnp.concatenate([q_ref[:, cols], k_ref[:, cols], v_ref[:, cols]], axis=1)
            base = pl.multiple_of(g * 8 * BOX, 8 * BOX)
            outbox[h, pl.ds(base, 8 * BOX), :] = dot(pick, rows).astype(BF16)
            if h < 2:
                send_boxes(h, g)
            return 0

        lax.fori_loop(0, 4, pack, 0)
        inbox[h, pl.ds(pl.multiple_of(my_seat * BOX, BOX), BOX), :] = outbox[h, 0:BOX, :]

    va[:, HD:] = jnp.ones((ROWS, HD), BF16)

    def wait_bytes(ref, semaphore):
        pltpu.make_async_copy(ref, ref, semaphore).wait()

    others = (PEERS - 1) * BOX

    def arrive(h):
        wait_bytes(inbox.at[h, pl.ds(0, others)], box_recv.at[h])
        if h == 0:
            wait_bytes(msg_in.at[pl.ds(0, PEERS - 1)], msg_recv)

        def prepare(s, _):
            base = pl.multiple_of(s * QUAD, QUAD)
            at = iota((BOX, SLOTS), 0).astype(F32)
            mine = iota((BOX, SLOTS), 1) // CL_DEV == me
            tags = []
            for j in range(4):
                low = msg_in[s * 4 + j, 2 * h : 2 * h + 1, :]
                high = msg_in[s * 4 + j, 2 * h + 1 : 2 * h + 2, :]
                tags.append(((at >= low) & (at < high) & mine).astype(BF16))
            tag = jnp.concatenate(tags, axis=0)
            box = inbox[h, pl.ds(base, QUAD), :]
            qa[pl.ds(base, QUAD), 0:HD] = box[:, 0:HD]
            qa[pl.ds(base, QUAD), HD:] = tag
            ka[pl.ds(base, QUAD), 0:HD] = box[:, HD : 2 * HD]
            ka[pl.ds(base, QUAD), HD:] = ((dot(tag, allow[h]) - 1.0) * BIG).astype(BF16)
            va[pl.ds(base, QUAD), 0:HD] = box[:, 2 * HD :]
            return 0

        lax.fori_loop(0, PEERS // 4, prepare, 0)

    def attend(h, low, high):
        def part(c, _):
            there_core, half = c // 2, (y // 2 + c % 2) % 2
            base = pl.multiple_of(seat(half * 2, 0, there_core) * BOX, 2 * QUAD)
            spans = [pl.ds(pl.multiple_of(base + i * QUAD, QUAD), QUAD) for i in range(2)]
            scores = [dot_t(qa[span, :], ka[...]) for span in spans]
            for i in range(2):
                top = jnp.max(scores[i], axis=1, keepdims=True)
                weights = jnp.exp2((scores[i] - top) * SCALE).astype(BF16)
                summed = dot(weights, va[...])
                ret_out[h, spans[i], :] = (summed[:, :HD] / summed[:, HD:]).astype(BF16)
            mine = pl.ds(pl.multiple_of(me * BOX, BOX), BOX)
            for j in range(8):
                there_y, there_x = half * 2 + (y + j) % 2, (x + j // 2) % 4
                rows = pl.ds(pl.multiple_of(seat(there_y, there_x, there_core) * BOX, BOX), BOX)

                def send(rows=rows, there_y=there_y, there_x=there_x):
                    pltpu.make_async_remote_copy(
                        src_ref=ret_out.at[h, rows],
                        dst_ref=ret_in.at[h, mine],
                        send_sem=ret_send.at[h],
                        recv_sem=ret_recv.at[h],
                        device_id=(device(there_y, there_x, there_core), plane),
                        device_id_type=MESH,
                    ).start()

                if j == 0:
                    self_here = (c % 2 == 0) & (there_core == core)
                    pl.when(jnp.logical_not(self_here))(send)

                    def keep(rows=rows):
                        ret_in[h, mine, :] = ret_out[h, rows, :]

                    pl.when(self_here)(keep)
                else:
                    send()
            return 0

        lax.fori_loop(low, high, part, 0)

    def gather_copy(h, step, c):
        rows = pl.ds(pl.multiple_of(c * QUAD, QUAD), QUAD)
        return pltpu.make_async_remote_copy(
            src_ref=att.at[h, plane, rows],
            dst_ref=att.at[h, plane, rows],
            send_sem=att_send.at[h, step - 1, c],
            recv_sem=att_recv.at[h, step - 1, c],
            device_id=(me, (plane + step) % PLANES),
            device_id_type=MESH,
        )

    def restore(h):
        wait_bytes(ret_in.at[h, pl.ds(0, others)], ret_recv.at[h])

        def tokens(c, _):
            base = pl.multiple_of(c * QUAD, QUAD)
            pos = pos_all[h, pl.ds(base, QUAD), :].astype(jnp.int32)
            lane = iota((QUAD, 128), 1)
            pick = jnp.concatenate(
                [(pos == lane + b * 128).astype(BF16) for b in range(ROWS // 128)], axis=1
            )
            att[h, plane, pl.ds(base, QUAD), :] = dot(pick, ret_in[h]).astype(BF16)
            for step in (2, 1, 3):
                gather_copy(h, step, c).start()
            return 0

        lax.fori_loop(0, TOK // QUAD, tokens, 0)

    def gathered(h, c):
        for step in range(1, PLANES):
            gather_copy(h, step, c).wait_recv()

    arrive(0)
    attend(0, 0, 4)
    send_late(0, 2)
    arrive(1)
    attend(1, 0, 4)
    send_late(2, 4)
    restore(0)
    restore(1)
    arrive(2)
    attend(2, 0, 3)
    pl.when(core == 0)(lambda: restore(2))
    attend(2, 3, 4)
    pl.when(core == 1)(lambda: restore(2))
    own_w.wait()
    for copy in w_copies:
        copy.wait()

    def project_two(c, _):
        rows = pl.ds(pl.multiple_of(c * QUAD, QUAD), QUAD)
        gathered(0, c)
        gathered(1, c)
        total = jnp.zeros((QUAD, OUT), F32)
        for p in range(PLANES):
            pair = jnp.concatenate([att[0, p, rows, :], att[1, p, rows, :]], axis=1)
            total = total + dot(pair, wcol[p, 0 : 2 * HD, :])
        acc[rows, :] = total
        return 0

    lax.fori_loop(0, TOK // QUAD, project_two, 0)

    def project_last(c, _):
        rows = pl.ds(pl.multiple_of(c * QUAD, QUAD), QUAD)
        gathered(2, c)
        total = acc[rows, :]
        for p in range(0, PLANES, 2):
            pair = jnp.concatenate([att[2, p, rows, :], att[2, p + 1, rows, :]], axis=1)
            both = jnp.concatenate([wcol[p, 2 * HD :, :], wcol[p + 1, 2 * HD :, :]], axis=0)
            total = total + dot(pair, both)
        out_ref[rows, :] = total.astype(BF16)
        return 0

    lax.fori_loop(0, TOK // QUAD, project_last, 0)

    for h in range(HEADS):
        wait_bytes(outbox.at[h, pl.ds(0, others)], box_send.at[h])
        wait_bytes(ret_out.at[h, pl.ds(0, others)], ret_send.at[h])
        for step in range(1, PLANES):
            for c in range(TOK // QUAD):
                gather_copy(h, step, c).wait_send()
    wait_bytes(msg_in.at[pl.ds(0, PEERS - 1)], msg_send)


def shards(queries, keys, values, clusters, cluster_slot, pair_shift, w_out):
    vmem = pl.BlockSpec(memory_space=pltpu.VMEM)
    dma = pltpu.SemaphoreType.DMA
    return pl.pallas_call(
        kernel,
        out_shape=jax.ShapeDtypeStruct((TOK, OUT), BF16),
        in_specs=[vmem] * 6 + [pl.BlockSpec(memory_space=pl.ANY)],
        out_specs=vmem,
        scratch_shapes=[
            pltpu.VMEM((HEADS, ROWS, 3 * HD), BF16),
            pltpu.VMEM((HEADS, ROWS, 3 * HD), BF16),
            pltpu.VMEM((8, SLOTS), F32),
            pltpu.VMEM((PEERS, 8, SLOTS), F32),
            pltpu.VMEM((HEADS, ROWS, HD), BF16),
            pltpu.VMEM((HEADS, ROWS, HD), BF16),
            pltpu.VMEM((HEADS, PLANES, TOK, HD), BF16),
            pltpu.VMEM((PLANES, HEADS * HD, OUT), BF16),
            pltpu.VMEM((TOK, OUT), F32),
            pltpu.VMEM((8, TOK), F32),
            pltpu.VMEM((HEADS, TOK, 128), F32),
            pltpu.VMEM((ROWS, 2 * HD), BF16),
            pltpu.VMEM((ROWS, 2 * HD), BF16),
            pltpu.VMEM((ROWS, 2 * HD), BF16),
            pltpu.VMEM((HEADS, SLOTS, SLOTS), BF16),
            dma((HEADS,)),
            dma((HEADS,)),
            dma,
            dma,
            dma((HEADS,)),
            dma((HEADS,)),
            dma((HEADS, PLANES - 1, TOK // QUAD)),
            dma((HEADS, PLANES - 1, TOK // QUAD)),
            dma((PLANES - 1,)),
            dma((PLANES - 1,)),
            dma,
        ],
        compiler_params=pltpu.CompilerParams(
            collective_id=0, has_side_effects=True, vmem_limit_bytes=62 * 2**20
        ),
        cost_estimate=pl.CostEstimate(
            flops=40 * 10**9, bytes_accessed=10 * 10**6, transcendentals=28 * 10**6
        ),
    )(queries, keys, values, clusters, cluster_slot, pair_shift, w_out)


def solution(mesh):
    in_specs = (
        P("tok", "head"),
        P("tok", "head"),
        P("tok", "head"),
        P("head", "tok"),
        P("head", None),
        P("head", None),
        P("head", None),
    )
    return jax.shard_map(
        shards, mesh=mesh, in_specs=in_specs, out_specs=P("tok", "head"), check_vma=False
    )
```

```python
import math

import jax
import jax.numpy as jnp
from jax import lax
from jax.experimental import pallas as pl
from jax.experimental.pallas import tpu as pltpu
from jax.sharding import PartitionSpec as P

HD = 128
CL_DEV = 4
SLOTS = 128
HEADS = 3
PEERS = 32
PLANES = 4
TOK = 1536
BOX = 96
ROWS = PEERS * BOX
OUT = 768
QUAD = 4 * BOX
BIG = 1e30
SCALE = math.log2(math.e) / math.sqrt(HD)
MESH = pl.DeviceIdType.MESH
DIRECT = (1,)
F32 = jnp.float32
BF16 = jnp.bfloat16


def iota(shape, dim):
    return lax.broadcasted_iota(jnp.int32, shape, dim)


def dot(left, right):
    return jnp.dot(left, right, preferred_element_type=F32)


def dot_t(left, right):
    return lax.dot_general(
        left, right, (((1,), (1,)), ((), ())), preferred_element_type=F32
    )


def kernel(
    q_hbm, k_hbm, v_hbm, cl_ref, slot_ref, shift_ref, w_ref, out_ref,
    q_ref, k_ref, v_ref, outbox, inbox, counts, ret_out, ret_in, att, wcol, acc,
    pos_row, pos_all, qa, ka, va, allow,
    box_send, box_recv, count_send, count_recv, ret_send, ret_recv,
    att_send, att_recv, w_send, w_recv, w_own, load,
):
    me = lax.axis_index("tok")
    plane = lax.axis_index("head")
    core, chip = me % 2, me // 2
    x, y = chip % 4, chip // 4

    def device(there_y, there_x, there_core):
        return (there_y * 4 + there_x) * 2 + there_core

    def seat(there_y, there_x, there_core):
        return there_core * 16 + there_y * 4 + there_x

    my_seat = seat(y, x, core)

    loads = []
    for i, (source, target) in enumerate(((q_hbm, q_ref), (k_hbm, k_ref), (v_hbm, v_ref))):
        loads.append(pltpu.make_async_copy(source, target, load.at[i]))
        loads[i].start()

    barrier = pltpu.get_barrier_semaphore()
    for step in range(1, PEERS):
        pl.semaphore_signal(
            barrier, inc=1, device_id=((me + step) % PEERS, plane), device_id_type=MESH
        )
    for step in range(1, PLANES):
        pl.semaphore_signal(
            barrier, inc=1, device_id=(me, (plane + step) % PLANES), device_id_type=MESH
        )

    below = (iota((128, 128), 0) <= iota((128, 128), 1)).astype(BF16)
    ones = jnp.ones((128, 128), BF16)
    row_id, col_id = iota((128, 128), 0), iota((128, 128), 1)
    same = row_id // CL_DEV == col_id // CL_DEV
    before = (same & (col_id < row_id)).astype(BF16)
    after = (same & (row_id < col_id)).astype(BF16)
    box_base = (row_id // CL_DEV * BOX - 1).astype(F32)

    def place(h):
        slot_line = slot_ref[h : h + 1, :]
        of_cluster = (iota((SLOTS, TOK), 0) == cl_ref[h : h + 1, :]).astype(BF16)
        slot_rows = jnp.broadcast_to(slot_line.astype(F32), (8, SLOTS)).astype(BF16)
        token_slot = dot(slot_rows, of_cluster)[0:1].astype(jnp.int32)
        hot = iota((SLOTS, TOK), 0) == token_slot
        hot_f, hot_b = hot.astype(F32), hot.astype(BF16)
        counted = jnp.zeros((128, 128), F32)
        within = []
        for b in range(TOK // 128):
            block = hot_b[:, b * 128 : (b + 1) * 128]
            within.append(dot(block, below) + counted)
            counted = counted + dot(block, ones)
        start = dot(before, counted.astype(BF16)) + box_base
        for b in range(TOK // 128):
            lanes = slice(b * 128, (b + 1) * 128)
            line = jnp.sum(hot_f[:, lanes] * (within[b] + start), axis=0, keepdims=True)
            pos_row[h : h + 1, lanes] = line
            pos_all[h, lanes, :] = jnp.broadcast_to(line, (128, 128)).T
        count_line = dot_t(jnp.ones((8, TOK), BF16), hot_b)
        low = dot(count_line.astype(BF16), after)
        counts[me, 2 * h : 2 * h + 1, :] = low[0:1]
        counts[me, 2 * h + 1 : 2 * h + 2, :] = (low + count_line)[0:1]
        placed = (row_id == slot_line).astype(BF16)
        shift_rows = jnp.broadcast_to(shift_ref[h : h + 1, :].astype(F32), (8, SLOTS))
        shift = dot_t(shift_rows.astype(BF16), placed)[0:1].astype(jnp.int32)
        mate = col_id // CL_DEV * CL_DEV + (col_id % CL_DEV + shift) % CL_DEV
        allow[h] = ((row_id == col_id) | (row_id == mate)).astype(BF16)
    def peer_of(g, j):
        return device((y + 2 * g + j // 4 + j) % 4, (x + j) % 4, (core + g // 2) % 2)

    def send_boxes(h, g):
        for j in range(8):
            def send(j=j):
                peer = (peer_of(g, j), plane)
                k = g * 8 + j
                pltpu.make_async_remote_copy(
                    src_ref=outbox.at[h, pl.ds(pl.multiple_of(k * BOX, BOX), BOX)],
                    dst_ref=inbox.at[h, pl.ds(pl.multiple_of(my_seat * BOX, BOX), BOX)],
                    send_sem=box_send.at[h],
                    recv_sem=box_recv.at[h],
                    device_id=peer,
                    device_id_type=MESH,
                ).start()

            if j == 0:
                pl.when(g != 0)(send)
            else:
                send()

    def send_late(low, high):
        def group(g, _):
            send_boxes(HEADS - 1, g)
            return 0

        lax.fori_loop(low, high, group, 0)

    def wait_bytes(ref, semaphore):
        pltpu.make_async_copy(ref, ref, semaphore).wait()

    others = (PEERS - 1) * BOX

    def count_copy(i):
        first, number, there = (
            (me, 1, device(y, x, 1 - core))
            if i == 0
            else (2 * chip, 2, device(y, (x + i) % 4, core))
            if i < 4
            else (8 * y, 8, device((y + i - 3) % 4, x, core))
        )
        return pltpu.make_async_remote_copy(
            src_ref=counts.at[pl.ds(first, number)],
            dst_ref=counts.at[pl.ds(first, number)],
            send_sem=count_send.at[i],
            recv_sem=count_recv.at[i],
            device_id=(there, plane),
            device_id_type=MESH,
        )

    def count_came(i):
        first, number = (
            (2 * chip + 1 - core, 1)
            if i == 0
            else (2 * (4 * y + (x + 4 - i) % 4), 2)
            if i < 4
            else (8 * ((y + 7 - i) % 4), 8)
        )
        wait_bytes(counts.at[pl.ds(first, number)], count_recv.at[i])

    def spread_counts(g):
        def along_x():
            count_came(0)
            for i in range(1, 4):
                count_copy(i).start()

        def along_y():
            for i in range(1, 4):
                count_came(i)
            for i in range(4, 7):
                count_copy(i).start()

        pl.when(g == 1)(along_x)
        pl.when(g == 3)(along_y)

    def fill(h):
        cols = slice(h * HD, (h + 1) * HD)

        def pack(g, _):
            if h == 0:
                spread_counts(g)
            pos = pos_row[h : h + 1, :].astype(jnp.int32)
            picks = []
            for j in range(8):
                picks.append((iota((BOX, TOK), 0) + peer_of(g, j) * BOX == pos).astype(BF16))
            pick = jnp.concatenate(picks, axis=0)
            rows = jnp.concatenate([q_ref[:, cols], k_ref[:, cols], v_ref[:, cols]], axis=1)
            base = pl.multiple_of(g * 8 * BOX, 8 * BOX)
            outbox[h, pl.ds(base, 8 * BOX), :] = dot(pick, rows).astype(BF16)
            if h < 2:
                send_boxes(h, g)
            return 0

        lax.fori_loop(0, 4, pack, 0)
        inbox[h, pl.ds(pl.multiple_of(my_seat * BOX, BOX), BOX), :] = outbox[h, 0:BOX, :]

    for h in range(HEADS):
        place(h)
    counts[me, 6:8, :] = jnp.zeros((2, SLOTS), F32)
    for copy in loads:
        copy.wait()
    pl.semaphore_wait(barrier, PEERS - 1 + PLANES - 1)
    count_copy(0).start()
    fill(0)
    own_w = pltpu.make_async_copy(
        w_ref.at[:, pl.ds(pl.multiple_of(plane * OUT, 128), OUT)], wcol.at[plane], w_own
    )
    own_w.start()
    w_copies = []
    for step in range(1, PLANES):
        there = (plane + step) % PLANES
        copy = pltpu.make_async_remote_copy(
            src_ref=w_ref.at[:, pl.ds(pl.multiple_of(there * OUT, 128), OUT)],
            dst_ref=wcol.at[plane],
            send_sem=w_send.at[step - 1],
            recv_sem=w_recv.at[step - 1],
            device_id=(me, there),
            device_id_type=MESH,
        )
        copy.start()
        w_copies.append(copy)

    fill(1)
    fill(2)

    va[:, HD:] = jnp.ones((ROWS, HD), BF16)

    def arrive(h):
        wait_bytes(inbox.at[h, pl.ds(0, others)], box_recv.at[h])

        def prepare(s, _):
            base = pl.multiple_of(s * QUAD, QUAD)
            at = iota((BOX, SLOTS), 0).astype(F32)
            mine = iota((BOX, SLOTS), 1) // CL_DEV == me
            tags = []
            for j in range(4):
                sender = device(s % 4, j, s // 4)
                low = counts[sender, 2 * h : 2 * h + 1, :]
                high = counts[sender, 2 * h + 1 : 2 * h + 2, :]
                tags.append(((at >= low) & (at < high) & mine).astype(BF16))
            tag = jnp.concatenate(tags, axis=0)
            box = inbox[h, pl.ds(base, QUAD), :]
            qa[pl.ds(base, QUAD), 0:HD] = box[:, 0:HD]
            qa[pl.ds(base, QUAD), HD:] = tag
            ka[pl.ds(base, QUAD), 0:HD] = box[:, HD : 2 * HD]
            ka[pl.ds(base, QUAD), HD:] = ((dot(tag, allow[h]) - 1.0) * BIG).astype(BF16)
            va[pl.ds(base, QUAD), 0:HD] = box[:, 2 * HD :]
            return 0

        lax.fori_loop(0, PEERS // 4, prepare, 0)

    def attend(h, hooks):
        def part(c, _):
            for at, when, hook in hooks:
                pl.when((c == at) & when)(hook)
            there_core, half = c // 2, (y // 2 + c % 2) % 2
            base = pl.multiple_of(seat(half * 2, 0, there_core) * BOX, 2 * QUAD)
            spans = [pl.ds(pl.multiple_of(base + i * QUAD, QUAD), QUAD) for i in range(2)]
            scores = [dot_t(qa[span, :], ka[...]) for span in spans]
            for i in range(2):
                top = jnp.max(scores[i], axis=1, keepdims=True)
                weights = jnp.exp2((scores[i] - top) * SCALE).astype(BF16)
                summed = dot(weights, va[...])
                ret_out[h, spans[i], :] = (summed[:, :HD] / summed[:, HD:]).astype(BF16)
            mine = pl.ds(pl.multiple_of(me * BOX, BOX), BOX)
            for j in range(8):
                there_y, there_x = half * 2 + (y + j) % 2, (x + j // 2) % 4
                rows = pl.ds(pl.multiple_of(seat(there_y, there_x, there_core) * BOX, BOX), BOX)

                def send(rows=rows, there_y=there_y, there_x=there_x):
                    pltpu.make_async_remote_copy(
                        src_ref=ret_out.at[h, rows],
                        dst_ref=ret_in.at[h, mine],
                        send_sem=ret_send.at[h],
                        recv_sem=ret_recv.at[h],
                        device_id=(device(there_y, there_x, there_core), plane),
                        device_id_type=MESH,
                    ).start()

                if j == 0:
                    self_here = (c % 2 == 0) & (there_core == core)
                    pl.when(jnp.logical_not(self_here))(send)

                    def keep(rows=rows):
                        ret_in[h, mine, :] = ret_out[h, rows, :]

                    pl.when(self_here)(keep)
                else:
                    send()
            return 0

        lax.fori_loop(0, 4, part, 0)

    left, right = (plane + PLANES - 1) % PLANES, (plane + 1) % PLANES
    half = QUAD // 2

    def gather_copy(h, way, c):
        first = c * QUAD + (half if way == 3 else 0)
        rows = pl.ds(pl.multiple_of(first, half), half if way >= 2 else QUAD)
        onward = way >= 2 and h not in DIRECT
        owner = (left, right)[way % 2] if onward else plane
        there = (plane + 2) % PLANES if way >= 2 and not onward else (right, left)[way % 2]
        return pltpu.make_async_remote_copy(
            src_ref=att.at[h, owner, rows],
            dst_ref=att.at[h, owner, rows],
            send_sem=att_send.at[h, way, c],
            recv_sem=att_recv.at[h, way, c],
            device_id=(me, there),
            device_id_type=MESH,
        )

    def forward(h, c):
        if h in DIRECT:
            return
        for way in range(2):
            gather_copy(h, way, c).wait_recv()
            gather_copy(h, way + 2, c).start()

    def forward_all(h):
        if h in DIRECT:
            return

        def one(c, _):
            forward(h, c)
            return 0

        lax.fori_loop(0, TOK // QUAD, one, 0)

    def restore(h):
        wait_bytes(ret_in.at[h, pl.ds(0, others)], ret_recv.at[h])

        def tokens(c, _):
            base = pl.multiple_of(c * QUAD, QUAD)
            pos = pos_all[h, pl.ds(base, QUAD), :].astype(jnp.int32)
            lane = iota((QUAD, 128), 1)
            pick = jnp.concatenate(
                [(pos == lane + b * 128).astype(BF16) for b in range(ROWS // 128)], axis=1
            )
            att[h, plane, pl.ds(base, QUAD), :] = dot(pick, ret_in[h]).astype(BF16)
            for way in range(4 if h in DIRECT else 2):
                gather_copy(h, way, c).start()
            return 0

        lax.fori_loop(0, TOK // QUAD, tokens, 0)

    def gathered(h, c):
        for way in range(0 if h in DIRECT else 2, 4):
            gather_copy(h, way, c).wait_recv()

    for i in range(4, 7):
        count_came(i)
    arrive(0)
    attend(0, [])
    send_late(0, 1)
    arrive(1)
    attend(1, [])
    send_late(1, 4)
    restore(0)
    own_w.wait()
    for copy in w_copies:
        copy.wait()
    forward_all(0)
    restore(1)
    arrive(2)
    attend(2, [])

    def project_two(c, _):
        rows = pl.ds(pl.multiple_of(c * QUAD, QUAD), QUAD)
        gathered(0, c)
        gathered(1, c)
        total = jnp.zeros((QUAD, OUT), F32)
        for p in range(PLANES):
            pair = jnp.concatenate([att[0, p, rows, :], att[1, p, rows, :]], axis=1)
            total = total + dot(pair, wcol[p, 0 : 2 * HD, :])
        acc[rows, :] = total
        return 0

    restore(2)
    forward_all(2)
    lax.fori_loop(0, TOK // QUAD, project_two, 0)

    def project_last(c, _):
        rows = pl.ds(pl.multiple_of(c * QUAD, QUAD), QUAD)
        gathered(2, c)
        total = acc[rows, :]
        for p in range(0, PLANES, 2):
            pair = jnp.concatenate([att[2, p, rows, :], att[2, p + 1, rows, :]], axis=1)
            both = jnp.concatenate([wcol[p, 2 * HD :, :], wcol[p + 1, 2 * HD :, :]], axis=0)
            total = total + dot(pair, both)
        out_ref[rows, :] = total.astype(BF16)
        return 0

    lax.fori_loop(0, TOK // QUAD, project_last, 0)

    for i in range(7):
        count_copy(i).wait_send()
    for h in range(HEADS):
        wait_bytes(outbox.at[h, pl.ds(0, others)], box_send.at[h])
        wait_bytes(ret_out.at[h, pl.ds(0, others)], ret_send.at[h])
        for way in range(4):
            for c in range(TOK // QUAD):
                gather_copy(h, way, c).wait_send()


def shards(queries, keys, values, clusters, cluster_slot, pair_shift, w_out):
    vmem = pl.BlockSpec(memory_space=pltpu.VMEM)
    hbm = pl.BlockSpec(memory_space=pl.ANY)
    dma = pltpu.SemaphoreType.DMA
    return pl.pallas_call(
        kernel,
        out_shape=jax.ShapeDtypeStruct((TOK, OUT), BF16),
        in_specs=[hbm] * 3 + [vmem] * 3 + [hbm],
        out_specs=vmem,
        scratch_shapes=[
            pltpu.VMEM((TOK, HEADS * HD), BF16),
            pltpu.VMEM((TOK, HEADS * HD), BF16),
            pltpu.VMEM((TOK, HEADS * HD), BF16),
            pltpu.VMEM((HEADS, ROWS, 3 * HD), BF16),
            pltpu.VMEM((HEADS, ROWS, 3 * HD), BF16),
            pltpu.VMEM((PEERS, 8, SLOTS), F32),
            pltpu.VMEM((HEADS, ROWS, HD), BF16),
            pltpu.VMEM((HEADS, ROWS, HD), BF16),
            pltpu.VMEM((HEADS, PLANES, TOK, HD), BF16),
            pltpu.VMEM((PLANES, HEADS * HD, OUT), BF16),
            pltpu.VMEM((TOK, OUT), F32),
            pltpu.VMEM((8, TOK), F32),
            pltpu.VMEM((HEADS, TOK, 128), F32),
            pltpu.VMEM((ROWS, 2 * HD), BF16),
            pltpu.VMEM((ROWS, 2 * HD), BF16),
            pltpu.VMEM((ROWS, 2 * HD), BF16),
            pltpu.VMEM((HEADS, SLOTS, SLOTS), BF16),
            dma((HEADS,)),
            dma((HEADS,)),
            dma((7,)),
            dma((7,)),
            dma((HEADS,)),
            dma((HEADS,)),
            dma((HEADS, 4, TOK // QUAD)),
            dma((HEADS, 4, TOK // QUAD)),
            dma((PLANES - 1,)),
            dma((PLANES - 1,)),
            dma,
            dma((3,)),
        ],
        compiler_params=pltpu.CompilerParams(
            collective_id=0, has_side_effects=True, vmem_limit_bytes=62 * 2**20
        ),
        cost_estimate=pl.CostEstimate(
            flops=40 * 10**9, bytes_accessed=10 * 10**6, transcendentals=28 * 10**6
        ),
    )(queries, keys, values, clusters, cluster_slot, pair_shift, w_out)


def solution(mesh):
    in_specs = (
        P("tok", "head"),
        P("tok", "head"),
        P("tok", "head"),
        P("head", "tok"),
        P("head", None),
        P("head", None),
        P("head", None),
    )
    return jax.shard_map(
        shards, mesh=mesh, in_specs=in_specs, out_specs=P("tok", "head"), check_vma=False
    )
```

```python
import math

import jax
import jax.numpy as jnp
from jax import lax
from jax.experimental import pallas as pl
from jax.experimental.pallas import tpu as pltpu
from jax.sharding import PartitionSpec as P

HD = 128
CL_DEV = 4
SLOTS = 128
HEADS = 3
PEERS = 32
PLANES = 4
TOK = 1536
BOX = 96
ROWS = PEERS * BOX
OUT = 768
QUAD = 4 * BOX
BIG = 1e30
SCALE = math.log2(math.e) / math.sqrt(HD)
MESH = pl.DeviceIdType.MESH
DIRECT = (1,)
F32 = jnp.float32
BF16 = jnp.bfloat16


def iota(shape, dim):
    return lax.broadcasted_iota(jnp.int32, shape, dim)


def dot(left, right):
    return jnp.dot(left, right, preferred_element_type=F32)


def dot_t(left, right):
    return lax.dot_general(
        left, right, (((1,), (1,)), ((), ())), preferred_element_type=F32
    )


def kernel(
    q_hbm, k_hbm, v_hbm, cl_ref, slot_ref, shift_ref, w_ref, out_ref,
    q_ref, k_ref, v_ref, outbox, inbox, counts, ret_out, ret_in, att, wcol, acc,
    pos_row, pos_all, qa, ka, va, allow,
    box_send, box_recv, count_send, count_recv, ret_send, ret_recv,
    att_send, att_recv, w_send, w_recv, w_own, load,
):
    me = lax.axis_index("tok")
    plane = lax.axis_index("head")
    core, chip = me % 2, me // 2
    x, y = chip % 4, chip // 4

    def device(there_y, there_x, there_core):
        return (there_y * 4 + there_x) * 2 + there_core

    def seat(there_y, there_x, there_core):
        return there_core * 16 + there_y * 4 + there_x

    my_seat = seat(y, x, core)

    loads = []
    for i, (source, target) in enumerate(((q_hbm, q_ref), (k_hbm, k_ref), (v_hbm, v_ref))):
        loads.append(pltpu.make_async_copy(source, target, load.at[i]))
        loads[i].start()

    barrier = pltpu.get_barrier_semaphore()
    for step in range(1, PEERS):
        pl.semaphore_signal(
            barrier, inc=1, device_id=((me + step) % PEERS, plane), device_id_type=MESH
        )
    for step in range(1, PLANES):
        pl.semaphore_signal(
            barrier, inc=1, device_id=(me, (plane + step) % PLANES), device_id_type=MESH
        )

    below = (iota((128, 128), 0) <= iota((128, 128), 1)).astype(BF16)
    ones = jnp.ones((128, 128), BF16)
    row_id, col_id = iota((128, 128), 0), iota((128, 128), 1)
    same = row_id // CL_DEV == col_id // CL_DEV
    before = (same & (col_id < row_id)).astype(BF16)
    after = (same & (row_id < col_id)).astype(BF16)
    box_base = (row_id // CL_DEV * BOX - 1).astype(F32)

    def place(h):
        slot_line = slot_ref[h : h + 1, :]
        of_cluster = (iota((SLOTS, TOK), 0) == cl_ref[h : h + 1, :]).astype(BF16)
        slot_rows = jnp.broadcast_to(slot_line.astype(F32), (8, SLOTS)).astype(BF16)
        token_slot = dot(slot_rows, of_cluster)[0:1].astype(jnp.int32)
        hot = iota((SLOTS, TOK), 0) == token_slot
        hot_f, hot_b = hot.astype(F32), hot.astype(BF16)
        counted = jnp.zeros((128, 128), F32)
        within = []
        for b in range(TOK // 128):
            block = hot_b[:, b * 128 : (b + 1) * 128]
            within.append(dot(block, below) + counted)
            counted = counted + dot(block, ones)
        start = dot(before, counted.astype(BF16)) + box_base
        for b in range(TOK // 128):
            lanes = slice(b * 128, (b + 1) * 128)
            line = jnp.sum(hot_f[:, lanes] * (within[b] + start), axis=0, keepdims=True)
            pos_row[h : h + 1, lanes] = line
            pos_all[h, lanes, :] = jnp.broadcast_to(line, (128, 128)).T
        count_line = dot_t(jnp.ones((8, TOK), BF16), hot_b)
        low = dot(count_line.astype(BF16), after)
        counts[me, 2 * h : 2 * h + 1, :] = low[0:1]
        counts[me, 2 * h + 1 : 2 * h + 2, :] = (low + count_line)[0:1]
        placed = (row_id == slot_line).astype(BF16)
        shift_rows = jnp.broadcast_to(shift_ref[h : h + 1, :].astype(F32), (8, SLOTS))
        shift = dot_t(shift_rows.astype(BF16), placed)[0:1].astype(jnp.int32)
        mate = col_id // CL_DEV * CL_DEV + (col_id % CL_DEV + shift) % CL_DEV
        allow[h] = ((row_id == col_id) | (row_id == mate)).astype(BF16)
    def peer_of(g, j):
        return device((y + 2 * g + j // 4 + j) % 4, (x + j) % 4, (core + g // 2) % 2)

    def send_boxes(h, g):
        for j in range(8):
            def send(j=j):
                peer = (peer_of(g, j), plane)
                k = g * 8 + j
                pltpu.make_async_remote_copy(
                    src_ref=outbox.at[h, pl.ds(pl.multiple_of(k * BOX, BOX), BOX)],
                    dst_ref=inbox.at[h, pl.ds(pl.multiple_of(my_seat * BOX, BOX), BOX)],
                    send_sem=box_send.at[h],
                    recv_sem=box_recv.at[h],
                    device_id=peer,
                    device_id_type=MESH,
                ).start()

            if j == 0:
                pl.when(g != 0)(send)
            else:
                send()

    def send_late(low, high):
        def group(g, _):
            send_boxes(HEADS - 1, g)
            return 0

        lax.fori_loop(low, high, group, 0)

    def wait_bytes(ref, semaphore):
        pltpu.make_async_copy(ref, ref, semaphore).wait()

    others = (PEERS - 1) * BOX

    def count_copy(i):
        first, number, there = (
            (me, 1, device(y, x, 1 - core))
            if i == 0
            else (2 * chip, 2, device(y, (x + i) % 4, core))
            if i < 4
            else (8 * y, 8, device((y + i - 3) % 4, x, core))
        )
        return pltpu.make_async_remote_copy(
            src_ref=counts.at[pl.ds(first, number)],
            dst_ref=counts.at[pl.ds(first, number)],
            send_sem=count_send.at[i],
            recv_sem=count_recv.at[i],
            device_id=(there, plane),
            device_id_type=MESH,
        )

    def count_came(i):
        first, number = (
            (2 * chip + 1 - core, 1)
            if i == 0
            else (2 * (4 * y + (x + 4 - i) % 4), 2)
            if i < 4
            else (8 * ((y + 7 - i) % 4), 8)
        )
        wait_bytes(counts.at[pl.ds(first, number)], count_recv.at[i])

    def spread_counts(g):
        def along_x():
            count_came(0)
            for i in range(1, 4):
                count_copy(i).start()

        def along_y():
            for i in range(1, 4):
                count_came(i)
            for i in range(4, 7):
                count_copy(i).start()

        pl.when(g == 1)(along_x)
        pl.when(g == 3)(along_y)

    def fill(h):
        cols = slice(h * HD, (h + 1) * HD)

        def pack(g, _):
            if h == 0:
                spread_counts(g)
            pos = pos_row[h : h + 1, :].astype(jnp.int32)
            picks = []
            for j in range(8):
                picks.append((iota((BOX, TOK), 0) + peer_of(g, j) * BOX == pos).astype(BF16))
            pick = jnp.concatenate(picks, axis=0)
            rows = jnp.concatenate([q_ref[:, cols], k_ref[:, cols], v_ref[:, cols]], axis=1)
            base = pl.multiple_of(g * 8 * BOX, 8 * BOX)
            outbox[h, pl.ds(base, 8 * BOX), :] = dot(pick, rows).astype(BF16)
            if h < 2:
                send_boxes(h, g)
            return 0

        lax.fori_loop(0, 4, pack, 0)
        inbox[h, pl.ds(pl.multiple_of(my_seat * BOX, BOX), BOX), :] = outbox[h, 0:BOX, :]

    for h in range(HEADS):
        place(h)
    counts[me, 6:8, :] = jnp.zeros((2, SLOTS), F32)
    for copy in loads:
        copy.wait()
    pl.semaphore_wait(barrier, PEERS - 1 + PLANES - 1)
    count_copy(0).start()
    fill(0)
    own_w = pltpu.make_async_copy(
        w_ref.at[:, pl.ds(pl.multiple_of(plane * OUT, 128), OUT)], wcol.at[plane], w_own
    )
    own_w.start()
    w_copies = []
    for step in range(1, PLANES):
        there = (plane + step) % PLANES
        copy = pltpu.make_async_remote_copy(
            src_ref=w_ref.at[:, pl.ds(pl.multiple_of(there * OUT, 128), OUT)],
            dst_ref=wcol.at[plane],
            send_sem=w_send.at[step - 1],
            recv_sem=w_recv.at[step - 1],
            device_id=(me, there),
            device_id_type=MESH,
        )
        copy.start()
        w_copies.append(copy)

    fill(1)
    fill(2)

    va[:, HD:] = jnp.ones((ROWS, HD), BF16)

    def arrive(h):
        wait_bytes(inbox.at[h, pl.ds(0, others)], box_recv.at[h])

        def prepare(s, _):
            base = pl.multiple_of(s * QUAD, QUAD)
            at = iota((BOX, SLOTS), 0).astype(F32)
            mine = iota((BOX, SLOTS), 1) // CL_DEV == me
            tags = []
            for j in range(4):
                sender = device(s % 4, j, s // 4)
                low = counts[sender, 2 * h : 2 * h + 1, :]
                high = counts[sender, 2 * h + 1 : 2 * h + 2, :]
                tags.append(((at >= low) & (at < high) & mine).astype(BF16))
            tag = jnp.concatenate(tags, axis=0)
            box = inbox[h, pl.ds(base, QUAD), :]
            qa[pl.ds(base, QUAD), 0:HD] = box[:, 0:HD]
            qa[pl.ds(base, QUAD), HD:] = tag
            ka[pl.ds(base, QUAD), 0:HD] = box[:, HD : 2 * HD]
            ka[pl.ds(base, QUAD), HD:] = ((dot(tag, allow[h]) - 1.0) * BIG).astype(BF16)
            va[pl.ds(base, QUAD), 0:HD] = box[:, 2 * HD :]
            return 0

        lax.fori_loop(0, PEERS // 4, prepare, 0)

    def attend(h, hooks):
        def part(c, _):
            for at, when, hook in hooks:
                pl.when((c == at) & when)(hook)
            there_core, half = c // 2, (y // 2 + c % 2) % 2
            base = pl.multiple_of(seat(half * 2, 0, there_core) * BOX, 2 * QUAD)
            spans = [pl.ds(pl.multiple_of(base + i * QUAD, QUAD), QUAD) for i in range(2)]
            scores = [dot_t(qa[span, :], ka[...]) for span in spans]
            for i in range(2):
                top = jnp.max(scores[i], axis=1, keepdims=True)
                weights = jnp.exp2((scores[i] - top) * SCALE).astype(BF16)
                summed = dot(weights, va[...])
                ret_out[h, spans[i], :] = (summed[:, :HD] / summed[:, HD:]).astype(BF16)
            mine = pl.ds(pl.multiple_of(me * BOX, BOX), BOX)
            for j in range(8):
                there_y, there_x = half * 2 + (y + j) % 2, (x + j // 2) % 4
                rows = pl.ds(pl.multiple_of(seat(there_y, there_x, there_core) * BOX, BOX), BOX)

                def send(rows=rows, there_y=there_y, there_x=there_x):
                    pltpu.make_async_remote_copy(
                        src_ref=ret_out.at[h, rows],
                        dst_ref=ret_in.at[h, mine],
                        send_sem=ret_send.at[h],
                        recv_sem=ret_recv.at[h],
                        device_id=(device(there_y, there_x, there_core), plane),
                        device_id_type=MESH,
                    ).start()

                if j == 0:
                    self_here = (c % 2 == 0) & (there_core == core)
                    pl.when(jnp.logical_not(self_here))(send)

                    def keep(rows=rows):
                        ret_in[h, mine, :] = ret_out[h, rows, :]

                    pl.when(self_here)(keep)
                else:
                    send()
            return 0

        lax.fori_loop(0, 4, part, 0)

    left, right = (plane + PLANES - 1) % PLANES, (plane + 1) % PLANES
    half = QUAD // 2

    def gather_copy(h, way, c):
        first = c * QUAD + (half if way == 3 else 0)
        rows = pl.ds(pl.multiple_of(first, half), half if way >= 2 else QUAD)
        onward = way >= 2 and h not in DIRECT
        owner = (left, right)[way % 2] if onward else plane
        there = (plane + 2) % PLANES if way >= 2 and not onward else (right, left)[way % 2]
        return pltpu.make_async_remote_copy(
            src_ref=att.at[h, owner, rows],
            dst_ref=att.at[h, owner, rows],
            send_sem=att_send.at[h, way, c],
            recv_sem=att_recv.at[h, way, c],
            device_id=(me, there),
            device_id_type=MESH,
        )

    def forward(h, c):
        if h in DIRECT:
            return
        for way in range(2):
            gather_copy(h, way, c).wait_recv()
            gather_copy(h, way + 2, c).start()

    def forward_all(h):
        if h in DIRECT:
            return

        def one(c, _):
            forward(h, c)
            return 0

        lax.fori_loop(0, TOK // QUAD, one, 0)

    def restore(h):
        wait_bytes(ret_in.at[h, pl.ds(0, others)], ret_recv.at[h])

        def tokens(c, _):
            base = pl.multiple_of(c * QUAD, QUAD)
            pos = pos_all[h, pl.ds(base, QUAD), :].astype(jnp.int32)
            lane = iota((QUAD, 128), 1)
            pick = jnp.concatenate(
                [(pos == lane + b * 128).astype(BF16) for b in range(ROWS // 128)], axis=1
            )
            att[h, plane, pl.ds(base, QUAD), :] = dot(pick, ret_in[h]).astype(BF16)
            for way in range(4 if h in DIRECT else 2):
                gather_copy(h, way, c).start()
            return 0

        lax.fori_loop(0, TOK // QUAD, tokens, 0)

    def gathered(h, c):
        for way in range(0 if h in DIRECT else 2, 4):
            gather_copy(h, way, c).wait_recv()

    for i in range(4, 7):
        count_came(i)
    arrive(0)
    attend(0, [])
    send_late(0, 1)
    arrive(1)
    attend(1, [(3, True, lambda: send_late(1, 4))])
    restore(0)
    own_w.wait()
    for copy in w_copies:
        copy.wait()
    forward_all(0)
    restore(1)
    arrive(2)
    attend(2, [])

    def project_two(c, _):
        rows = pl.ds(pl.multiple_of(c * QUAD, QUAD), QUAD)
        gathered(0, c)
        gathered(1, c)
        total = jnp.zeros((QUAD, OUT), F32)
        for p in range(PLANES):
            pair = jnp.concatenate([att[0, p, rows, :], att[1, p, rows, :]], axis=1)
            total = total + dot(pair, wcol[p, 0 : 2 * HD, :])
        acc[rows, :] = total
        return 0

    restore(2)
    forward_all(2)
    lax.fori_loop(0, TOK // QUAD, project_two, 0)

    def project_last(c, _):
        rows = pl.ds(pl.multiple_of(c * QUAD, QUAD), QUAD)
        gathered(2, c)
        total = acc[rows, :]
        for p in range(0, PLANES, 2):
            pair = jnp.concatenate([att[2, p, rows, :], att[2, p + 1, rows, :]], axis=1)
            both = jnp.concatenate([wcol[p, 2 * HD :, :], wcol[p + 1, 2 * HD :, :]], axis=0)
            total = total + dot(pair, both)
        out_ref[rows, :] = total.astype(BF16)
        return 0

    lax.fori_loop(0, TOK // QUAD, project_last, 0)

    for i in range(7):
        count_copy(i).wait_send()
    for h in range(HEADS):
        wait_bytes(outbox.at[h, pl.ds(0, others)], box_send.at[h])
        wait_bytes(ret_out.at[h, pl.ds(0, others)], ret_send.at[h])
        for way in range(4):
            for c in range(TOK // QUAD):
                gather_copy(h, way, c).wait_send()


def shards(queries, keys, values, clusters, cluster_slot, pair_shift, w_out):
    vmem = pl.BlockSpec(memory_space=pltpu.VMEM)
    hbm = pl.BlockSpec(memory_space=pl.ANY)
    dma = pltpu.SemaphoreType.DMA
    return pl.pallas_call(
        kernel,
        out_shape=jax.ShapeDtypeStruct((TOK, OUT), BF16),
        in_specs=[hbm] * 3 + [vmem] * 3 + [hbm],
        out_specs=vmem,
        scratch_shapes=[
            pltpu.VMEM((TOK, HEADS * HD), BF16),
            pltpu.VMEM((TOK, HEADS * HD), BF16),
            pltpu.VMEM((TOK, HEADS * HD), BF16),
            pltpu.VMEM((HEADS, ROWS, 3 * HD), BF16),
            pltpu.VMEM((HEADS, ROWS, 3 * HD), BF16),
            pltpu.VMEM((PEERS, 8, SLOTS), F32),
            pltpu.VMEM((HEADS, ROWS, HD), BF16),
            pltpu.VMEM((HEADS, ROWS, HD), BF16),
            pltpu.VMEM((HEADS, PLANES, TOK, HD), BF16),
            pltpu.VMEM((PLANES, HEADS * HD, OUT), BF16),
            pltpu.VMEM((TOK, OUT), F32),
            pltpu.VMEM((8, TOK), F32),
            pltpu.VMEM((HEADS, TOK, 128), F32),
            pltpu.VMEM((ROWS, 2 * HD), BF16),
            pltpu.VMEM((ROWS, 2 * HD), BF16),
            pltpu.VMEM((ROWS, 2 * HD), BF16),
            pltpu.VMEM((HEADS, SLOTS, SLOTS), BF16),
            dma((HEADS,)),
            dma((HEADS,)),
            dma((7,)),
            dma((7,)),
            dma((HEADS,)),
            dma((HEADS,)),
            dma((HEADS, 4, TOK // QUAD)),
            dma((HEADS, 4, TOK // QUAD)),
            dma((PLANES - 1,)),
            dma((PLANES - 1,)),
            dma,
            dma((3,)),
        ],
        compiler_params=pltpu.CompilerParams(
            collective_id=0, has_side_effects=True, vmem_limit_bytes=62 * 2**20
        ),
        cost_estimate=pl.CostEstimate(
            flops=40 * 10**9, bytes_accessed=10 * 10**6, transcendentals=28 * 10**6
        ),
    )(queries, keys, values, clusters, cluster_slot, pair_shift, w_out)


def solution(mesh):
    in_specs = (
        P("tok", "head"),
        P("tok", "head"),
        P("tok", "head"),
        P("head", "tok"),
        P("head", None),
        P("head", None),
        P("head", None),
    )
    return jax.shard_map(
        shards, mesh=mesh, in_specs=in_specs, out_specs=P("tok", "head"), check_vma=False
    )
```
